32 devices in a mesh: groups: 2 (over y), tp: 4 (over z), dp: 4 (over x, core).
Axes of the slice: x: 2, y: 2, z: 4, core: 2. Of those that a mesh axis runs over, the one named last changes fastest.
Arguments:
- tokens: bfloat16 [256, 7168], P(('groups', 'tp'), 'dp'), parts along dimension 0, may hold values from -6 to 6
- counts: int32 [8], P(('groups', 'tp')), parts along dimension 0, may hold values from 0 to 32, as said below
- gate_weight: bfloat16 [7168, 18432], P('dp', 'tp'), may hold values from -0.0625 to 0.0625
- up_weight: bfloat16 [7168, 18432], P('dp', 'tp'), may hold values from -0.0625 to 0.0625
- down_weight: bfloat16 [18432, 7168], P('tp', 'dp'), may hold values from -0.046875 to 0.046875
Outputs:
- mixed: bfloat16 [256, 7168], P(('groups', 'tp'), 'dp'), parts along dimension 0
The draws below stay inside these ranges and needn't reach their ends.
There are 2 independent parts, one for each index of `groups`. The reference program is written for one: setup_inputs(seed, part) draws one part's arguments, and reference() takes and returns one part's arrays. A program takes and returns all parts, laid end to end along the dimension named above; an argument that names none is the same for every part. Nothing has to cross between parts.
Inputs may be any that keep to these rules, and one draw needn't show every extreme that they name: `counts`: some attention rank has all 32 slots live in every draw.
All inputs are finite; a program needn't handle non-finite values.
Results may differ from the reference program's by a relative error of at most 0.005.
Values may be sent and summed in bfloat16 or wider, within the bound.
A program may use at most 128 MiB of HBM per device.

```python
import jax
import jax.numpy as jnp

D = 7168
FF = 18432
ROWS = 32
RANKS = 4
ROW_TOTAL = 128


def draw_counts(key, part):
    key = jax.random.fold_in(key, 7)
    first, second = jax.random.split(key)
    values = jax.random.randint(first, (RANKS,), 0, ROWS + 1)
    full_rank = jax.random.randint(second, (), 0, RANKS)
    return jnp.where(jnp.arange(RANKS) == full_rank, ROWS, values).astype(jnp.int32)


def levels(rng, dims, cuts, least, top_value):
    gain = 1.0
    for dim, parts in cuts:
        heights = jax.random.uniform(jax.random.fold_in(jax.random.fold_in(rng, 6), dim), (parts,), jnp.float32, least / len(cuts), top_value / len(cuts))
        gain = gain * jnp.repeat(jnp.exp(heights), dims[dim] // parts).reshape((-1,) + (1,) * (len(dims) - 1 - dim))
    return gain


def normal_values(stream_key, extent, spread, most, cuts=(), kind=jnp.bfloat16):
    drawn = spread * jax.random.normal(stream_key, extent, jnp.float32)
    if cuts:
        drawn = drawn * levels(stream_key, extent, cuts, -0.22, 0.18)
    return jnp.clip(drawn, -most, most).astype(kind)


def setup_inputs(seed: int = 0, part: int = 0) -> dict:
    splits = jax.random.split(jax.random.key(seed), 6)
    own_keys = jax.random.split(jax.random.fold_in(splits[5], part), 6)
    tokens = normal_values(own_keys[0], (ROW_TOTAL, D), 1.0, 6.0, ((0, 4), (1, 4)))
    counts = draw_counts(jax.random.fold_in(jax.random.fold_in(splits[5], part), 71), part)
    gate_weight = normal_values(splits[2], (D, FF), D ** -0.5, 0.0625, ((0, 4), (1, 4)))
    up_weight = normal_values(splits[3], (D, FF), D ** -0.5, 0.0625, ((0, 4), (1, 4)))
    down_weight = normal_values(splits[4], (FF, D), FF ** -0.5, 0.046875, ((0, 4), (1, 4)))
    return {"tokens": tokens, "counts": counts, "gate_weight": gate_weight, "up_weight": up_weight, "down_weight": down_weight}


def reference(tokens, counts, gate_weight, up_weight, down_weight):
    gate = jnp.dot(tokens, gate_weight, preferred_element_type=jnp.float32)
    up = jnp.dot(tokens, up_weight, preferred_element_type=jnp.float32)
    hidden = (jax.nn.silu(gate) * up).astype(jnp.bfloat16)
    product = jnp.dot(hidden, down_weight, preferred_element_type=jnp.float32)
    row_index = jnp.arange(ROW_TOTAL, dtype=jnp.int32)
    live = (row_index % ROWS) < counts[row_index // ROWS]
    return jnp.where(live[:, None], product, jnp.float32(0.0)).astype(jnp.bfloat16)
```

```python
import functools

import jax
import jax.numpy as jnp
from jax import lax
from jax.experimental import pallas as pl
from jax.experimental.pallas import tpu as pltpu
from jax.sharding import PartitionSpec as P

MESH = pl.DeviceIdType.MESH
SLOTS = 3


def chunk_of(units):
    for width in (512, 384, 256, 128):
        if units % width == 0:
            return width
    return units


def kernel(
    n_tp, n_dp, n, width,
    tokens, gate_w, up_w, down_w, out,
    rows_all, gate_v, up_v, down_v, part, core_in, own, x_out, x_in, hidden, product, z_out, z_in,
    tok_local, tok_s, tok_r, gate_s, up_s, down_s, core_s, core_r, x_s, x_r,
    ag_s, ag_r, sib_s, sib_r, fwd_s, fwd_r, z_s, z_r,
):
    rank = lax.axis_index("tp")
    dp = lax.axis_index("dp")
    n_x = n_dp // 2
    x, core = lax.div(dp, 2), lax.rem(dp, 2)
    sibling = x * 2 + 1 - core
    slots = tokens.shape[0]
    share = slots * n_tp // n_dp

    def x_peer(d):
        return lax.rem(x + d, n_x) * 2 + core

    def block(index, size):
        return pl.ds(pl.multiple_of(index * size, size), size)

    def weight_copies(k):
        columns = pl.ds(pl.multiple_of(k * width, width), width) if n > 1 else pl.ds(0, width)
        return (
            pltpu.make_async_copy(gate_w.at[:, columns], gate_v.at[k], gate_s.at[k]),
            pltpu.make_async_copy(up_w.at[:, columns], up_v.at[k], up_s.at[k]),
        )

    def down_copy(k):
        rows = pl.ds(pl.multiple_of(k * width, width), width) if n > 1 else pl.ds(0, width)
        return pltpu.make_async_copy(down_w.at[rows, :], down_v.at[k], down_s.at[k])

    def token_copy(d):
        return pltpu.make_async_remote_copy(
            src_ref=tokens, dst_ref=rows_all.at[block(rank, slots)],
            send_sem=tok_s.at[d - 1], recv_sem=tok_r.at[d - 1],
            device_id={"tp": lax.rem(rank + d, n_tp)}, device_id_type=MESH,
        )

    def token_arrival(d):
        return pltpu.make_async_remote_copy(
            src_ref=tokens, dst_ref=rows_all.at[block(lax.rem(rank + n_tp - d, n_tp), slots)],
            send_sem=tok_s.at[d - 1], recv_sem=tok_r.at[d - 1],
            device_id={"tp": lax.rem(rank + d, n_tp)}, device_id_type=MESH,
        )

    def core_copy(k, i):
        return pltpu.make_async_remote_copy(
            src_ref=part.at[lax.rem(k, SLOTS), :, block(i * 2 + 1 - core, share), :],
            dst_ref=core_in.at[k, i],
            send_sem=core_s.at[k, i], recv_sem=core_r.at[k, i],
            device_id={"dp": sibling}, device_id_type=MESH,
        )

    def x_copy(k, d):
        return pltpu.make_async_remote_copy(
            src_ref=x_out.at[k, d - 1], dst_ref=x_in.at[k, d - 1],
            send_sem=x_s.at[k, d - 1], recv_sem=x_r.at[k, d - 1],
            device_id={"dp": x_peer(d)}, device_id_type=MESH,
        )

    def hidden_copy(k, owner, target, send, recv):
        ref = hidden.at[k, block(owner, share), :]
        return pltpu.make_async_remote_copy(
            src_ref=ref, dst_ref=ref, send_sem=send, recv_sem=recv,
            device_id={"dp": target}, device_id_type=MESH,
        )

    def ag_copy(k, d):
        return hidden_copy(k, dp, x_peer(d), ag_s.at[k, d - 1], ag_r.at[k, d - 1])

    def ag_arrival(k, d):
        return hidden_copy(k, x_peer(n_x - d), x_peer(d), ag_s.at[k, d - 1], ag_r.at[k, d - 1])

    def sib_copy(k):
        return hidden_copy(k, dp, sibling, sib_s.at[k], sib_r.at[k])

    def sib_arrival(k):
        return hidden_copy(k, sibling, sibling, sib_s.at[k], sib_r.at[k])

    def fwd_copy(k, d):
        return hidden_copy(k, x_peer(n_x - d), sibling, fwd_s.at[k, d - 1], fwd_r.at[k, d - 1])

    def fwd_arrival(k, d):
        owner = lax.rem(x + n_x - d, n_x) * 2 + 1 - core
        return hidden_copy(k, owner, sibling, fwd_s.at[k, d - 1], fwd_r.at[k, d - 1])

    def z_copy(d):
        return pltpu.make_async_remote_copy(
            src_ref=z_out.at[d - 1], dst_ref=z_in.at[d - 1],
            send_sem=z_s.at[d - 1], recv_sem=z_r.at[d - 1],
            device_id={"tp": lax.rem(rank + d, n_tp)}, device_id_type=MESH,
        )

    own_rows = pltpu.make_async_copy(tokens, rows_all.at[block(rank, slots)], tok_local)
    own_rows.start()

    barrier = pltpu.get_barrier_semaphore()
    for d in range(1, n_tp):
        pl.semaphore_signal(barrier, inc=1, device_id={"tp": lax.rem(rank + d, n_tp)}, device_id_type=MESH)
    for d in range(1, n_x):
        pl.semaphore_signal(barrier, inc=1, device_id={"dp": x_peer(d)}, device_id_type=MESH)
    pl.semaphore_signal(barrier, inc=1, device_id={"dp": sibling}, device_id_type=MESH)

    @pl.loop(0, n)
    def _(k):
        for copy in weight_copies(k):
            copy.start()

    pl.semaphore_wait(barrier, n_tp - 1 + n_x)
    for d in range(1, n_tp):
        token_copy(d).start()

    @pl.loop(0, n)
    def _(k):
        down_copy(k).start()

    product[...] = jnp.zeros_like(product)
    own_rows.wait()
    for d in range(1, n_tp):
        token_arrival(d).wait_recv()

    @pl.loop(0, n + 4)
    def _(k):
        @pl.when(k < n)
        def _():
            @pl.when(k >= SLOTS)
            def _():
                for i in range(n_x):
                    core_copy(k - SLOTS, i).wait_send()

            slot = lax.rem(k, SLOTS)
            first, second = weight_copies(k)
            first.wait()
            part[slot, 0] = jnp.dot(rows_all[...], gate_v[k], preferred_element_type=jnp.float32)
            second.wait()
            part[slot, 1] = jnp.dot(rows_all[...], up_v[k], preferred_element_type=jnp.float32)
            for i in range(n_x):
                core_copy(k, i).start()

        @pl.when((k >= 1) & (k <= n))
        def _():
            j = k - 1
            slot = lax.rem(j, SLOTS)
            for i in range(n_x):
                core_copy(j, i).wait_recv()
            for d in range(1, n_x):
                to = lax.rem(x + d, n_x)
                for g in range(2):
                    x_out[j, d - 1, g] = (
                        part[slot, g, block(to * 2 + core, share), :] + core_in[j, to, g]
                    ).astype(jnp.bfloat16)
                x_copy(j, d).start()
            for g in range(2):
                own[lax.rem(j, 2), g] = part[slot, g, block(dp, share), :] + core_in[j, x, g]

        @pl.when((k >= 2) & (k <= n + 1))
        def _():
            j = k - 2
            for d in range(1, n_x):
                x_copy(j, d).wait_recv()
            gate, up = own[lax.rem(j, 2), 0], own[lax.rem(j, 2), 1]
            for d in range(1, n_x):
                gate += x_in[j, d - 1, 0].astype(jnp.float32)
                up += x_in[j, d - 1, 1].astype(jnp.float32)
            hidden[j, block(dp, share), :] = (gate / (1.0 + jnp.exp(-gate)) * up).astype(jnp.bfloat16)
            for d in range(1, n_x):
                ag_copy(j, d).start()
            sib_copy(j).start()

        @pl.when((k >= 3) & (k <= n + 2))
        def _():
            j = k - 3
            for d in range(1, n_x):
                ag_arrival(j, d).wait_recv()
                fwd_copy(j, d).start()

        @pl.when(k >= 4)
        def _():
            j = k - 4
            sib_arrival(j).wait_recv()
            for d in range(1, n_x):
                fwd_arrival(j, d).wait_recv()
            down_copy(j).wait()
            product[...] += jnp.dot(hidden[j], down_v[j], preferred_element_type=jnp.float32)

    for d in range(1, n_tp):
        z_out[d - 1] = product[block(lax.rem(rank + d, n_tp), slots), :].astype(jnp.bfloat16)
        z_copy(d).start()

    for d in range(1, n_tp):
        token_copy(d).wait_send()

    @pl.loop(0, n)
    def _(k):
        @pl.when(k + SLOTS >= n)
        def _():
            for i in range(n_x):
                core_copy(k, i).wait_send()
        for d in range(1, n_x):
            x_copy(k, d).wait_send()
            ag_copy(k, d).wait_send()
            fwd_copy(k, d).wait_send()
        sib_copy(k).wait_send()

    total = product[block(rank, slots), :]
    for d in range(1, n_tp):
        z_copy(d).wait_recv()
        total += z_in[d - 1].astype(jnp.float32)
    out[...] = total.astype(jnp.bfloat16)
    for d in range(1, n_tp):
        z_copy(d).wait_send()


def solution(mesh):
    n_tp, n_dp = mesh.shape["tp"], mesh.shape["dp"]
    n_x = n_dp // 2

    def on_device(tokens, counts, gate_weight, up_weight, down_weight):
        slots, depth = tokens.shape
        units = gate_weight.shape[1]
        width = chunk_of(units)
        n = units // width
        rows = slots * n_tp
        share = rows // n_dp
        far = max(n_x - 1, 1)
        dma = pltpu.SemaphoreType.DMA
        mixed = pl.pallas_call(
            functools.partial(kernel, n_tp, n_dp, n, width),
            out_shape=jax.ShapeDtypeStruct((slots, depth), jnp.bfloat16),
            in_specs=[pl.BlockSpec(memory_space=pl.ANY)] * 4,
            out_specs=pl.BlockSpec(memory_space=pltpu.VMEM),
            scratch_shapes=[
                pltpu.VMEM((rows, depth), jnp.bfloat16),
                pltpu.VMEM((n, depth, width), jnp.bfloat16),
                pltpu.VMEM((n, depth, width), jnp.bfloat16),
                pltpu.VMEM((n, width, depth), jnp.bfloat16),
                pltpu.VMEM((SLOTS, 2, rows, width), jnp.float32),
                pltpu.VMEM((n, n_x, 2, share, width), jnp.float32),
                pltpu.VMEM((2, 2, share, width), jnp.float32),
                pltpu.VMEM((n, far, 2, share, width), jnp.bfloat16),
                pltpu.VMEM((n, far, 2, share, width), jnp.bfloat16),
                pltpu.VMEM((n, rows, width), jnp.bfloat16),
                pltpu.VMEM((rows, depth), jnp.float32),
                pltpu.VMEM((n_tp - 1, slots, depth), jnp.bfloat16),
                pltpu.VMEM((n_tp - 1, slots, depth), jnp.bfloat16),
                dma, dma((n_tp - 1,)), dma((n_tp - 1,)),
                dma((n,)), dma((n,)), dma((n,)),
                dma((n, n_x)), dma((n, n_x)), dma((n, far)), dma((n, far)),
                dma((n, far)), dma((n, far)), dma((n,)), dma((n,)), dma((n, far)), dma((n, far)),
                dma((n_tp - 1,)), dma((n_tp - 1,)),
            ],
            compiler_params=pltpu.CompilerParams(
                collective_id=0, has_side_effects=True, vmem_limit_bytes=62 * 1024 * 1024
            ),
        )(tokens, gate_weight, up_weight, down_weight)
        live = jnp.arange(slots, dtype=jnp.int32) < counts[0]
        return jnp.where(live[:, None], mixed, jnp.bfloat16(0.0))

    in_specs = (
        P(("groups", "tp"), "dp"),
        P(("groups", "tp")),
        P("dp", "tp"),
        P("dp", "tp"),
        P("tp", "dp"),
    )
    return jax.shard_map(
        on_device, mesh=mesh, in_specs=in_specs, out_specs=P(("groups", "tp"), "dp"), check_vma=False
    )
```

```python
import functools

import jax
import jax.numpy as jnp
from jax import lax
from jax.experimental import pallas as pl
from jax.experimental.pallas import tpu as pltpu
from jax.sharding import PartitionSpec as P

MESH = pl.DeviceIdType.MESH
SLOTS = 4
LAG = 2
HALVES = 2


def chunk_of(units):
    for width in (768, 512, 384, 256, 128):
        if units % width == 0:
            return width
    return units


def kernel(
    n_tp, n_dp, n, width,
    tokens, gate_w, up_w, down_w, out,
    rows_all, gate_v, up_v, down_v, part, core_in, own, x_out, x_in, hidden, product, z_out, z_in,
    tok_local, tok_s, tok_r, gate_s, up_s, down_s, core_s, core_r, x_s, x_r,
    ag_s, ag_r, sib_s, sib_r, fwd_s, fwd_r, z_s, z_r,
):
    rank = lax.axis_index("tp")
    dp = lax.axis_index("dp")
    n_x = n_dp // 2
    x, core = lax.div(dp, 2), lax.rem(dp, 2)
    sibling = x * 2 + 1 - core
    slots = tokens.shape[0] // HALVES
    share = slots * n_tp // n_dp
    steps = HALVES * n

    def x_peer(d):
        return lax.rem(x + d, n_x) * 2 + core

    def block(index, size):
        return pl.ds(pl.multiple_of(index * size, size), size)

    def weight_copies(k):
        columns = pl.ds(pl.multiple_of(k * width, width), width) if n > 1 else pl.ds(0, width)
        return (
            pltpu.make_async_copy(gate_w.at[:, columns], gate_v.at[k], gate_s.at[k]),
            pltpu.make_async_copy(up_w.at[:, columns], up_v.at[k], up_s.at[k]),
        )

    def down_copy(k):
        rows = pl.ds(pl.multiple_of(k * width, width), width) if n > 1 else pl.ds(0, width)
        return pltpu.make_async_copy(down_w.at[rows, :], down_v.at[k], down_s.at[k])

    def token_move(h, d, source):
        return pltpu.make_async_remote_copy(
            src_ref=tokens.at[pl.ds(h * slots, slots)], dst_ref=rows_all.at[h, block(source, slots)],
            send_sem=tok_s.at[h, d - 1], recv_sem=tok_r.at[h, d - 1],
            device_id={"tp": lax.rem(rank + d, n_tp)}, device_id_type=MESH,
        )

    def token_copy(h, d):
        return token_move(h, d, rank)

    def token_arrival(h, d):
        return token_move(h, d, lax.rem(rank + n_tp - d, n_tp))

    def core_copy(k, i):
        return pltpu.make_async_remote_copy(
            src_ref=part.at[lax.rem(k, SLOTS), :, block(i * 2 + 1 - core, share), :],
            dst_ref=core_in.at[k, i],
            send_sem=core_s.at[k, i], recv_sem=core_r.at[k, i],
            device_id={"dp": sibling}, device_id_type=MESH,
        )

    def x_copy(k, d):
        return pltpu.make_async_remote_copy(
            src_ref=x_out.at[k, d - 1], dst_ref=x_in.at[k, d - 1],
            send_sem=x_s.at[k, d - 1], recv_sem=x_r.at[k, d - 1],
            device_id={"dp": x_peer(d)}, device_id_type=MESH,
        )

    def hidden_copy(k, owner, target, send, recv):
        ref = hidden.at[k, block(owner, share), :]
        return pltpu.make_async_remote_copy(
            src_ref=ref, dst_ref=ref, send_sem=send, recv_sem=recv,
            device_id={"dp": target}, device_id_type=MESH,
        )

    def ag_copy(k, d):
        return hidden_copy(k, dp, x_peer(d), ag_s.at[k, d - 1], ag_r.at[k, d - 1])

    def ag_arrival(k, d):
        return hidden_copy(k, x_peer(n_x - d), x_peer(d), ag_s.at[k, d - 1], ag_r.at[k, d - 1])

    def sib_copy(k):
        return hidden_copy(k, dp, sibling, sib_s.at[k], sib_r.at[k])

    def sib_arrival(k):
        return hidden_copy(k, sibling, sibling, sib_s.at[k], sib_r.at[k])

    def fwd_copy(k, d):
        return hidden_copy(k, x_peer(n_x - d), sibling, fwd_s.at[k, d - 1], fwd_r.at[k, d - 1])

    def fwd_arrival(k, d):
        owner = lax.rem(x + n_x - d, n_x) * 2 + 1 - core
        return hidden_copy(k, owner, sibling, fwd_s.at[k, d - 1], fwd_r.at[k, d - 1])

    def z_copy(h, d):
        return pltpu.make_async_remote_copy(
            src_ref=z_out.at[h, d - 1], dst_ref=z_in.at[h, d - 1],
            send_sem=z_s.at[h, d - 1], recv_sem=z_r.at[h, d - 1],
            device_id={"tp": lax.rem(rank + d, n_tp)}, device_id_type=MESH,
        )

    def send_product(h):
        for d in range(1, n_tp):
            z_out[h, d - 1] = product[h, block(lax.rem(rank + d, n_tp), slots), :].astype(jnp.bfloat16)
            z_copy(h, d).start()

    own_rows = [
        pltpu.make_async_copy(
            tokens.at[pl.ds(h * slots, slots)], rows_all.at[h, block(rank, slots)], tok_local.at[h]
        )
        for h in range(HALVES)
    ]
    for copy in own_rows:
        copy.start()

    barrier = pltpu.get_barrier_semaphore()
    for d in range(1, n_tp):
        pl.semaphore_signal(barrier, inc=1, device_id={"tp": lax.rem(rank + d, n_tp)}, device_id_type=MESH)
    for d in range(1, n_x):
        pl.semaphore_signal(barrier, inc=1, device_id={"dp": x_peer(d)}, device_id_type=MESH)
    pl.semaphore_signal(barrier, inc=1, device_id={"dp": sibling}, device_id_type=MESH)

    @pl.loop(0, n)
    def _(k):
        for copy in weight_copies(k):
            copy.start()

    pl.semaphore_wait(barrier, n_tp - 1 + n_x)
    for d in range(1, n_tp):
        token_copy(0, d).start()

    @pl.loop(0, n)
    def _(k):
        down_copy(k).start()

    product[...] = jnp.zeros_like(product)
    for copy in own_rows:
        copy.wait()
    for d in range(1, n_tp):
        token_arrival(0, d).wait_recv()
    for h in range(1, HALVES):
        for d in range(1, n_tp):
            token_copy(h, d).start()

    @pl.loop(0, steps + 4 * LAG)
    def _(k):
        @pl.when(k < steps)
        def _():
            @pl.when(k >= SLOTS)
            def _():
                for i in range(n_x):
                    core_copy(k - SLOTS, i).wait_send()

            for h in range(1, HALVES):
                @pl.when(k == h * n)
                def _():
                    for d in range(1, n_tp):
                        token_arrival(h, d).wait_recv()

            slot, h, c = lax.rem(k, SLOTS), lax.div(k, n), lax.rem(k, n)

            @pl.when(k < n)
            def _():
                for copy in weight_copies(c):
                    copy.wait()

            part[slot, 0] = jnp.dot(rows_all[h], gate_v[c], preferred_element_type=jnp.float32)
            part[slot, 1] = jnp.dot(rows_all[h], up_v[c], preferred_element_type=jnp.float32)
            for i in range(n_x):
                core_copy(k, i).start()

        @pl.when((k >= LAG) & (k < steps + LAG))
        def _():
            j = k - LAG
            slot = lax.rem(j, SLOTS)
            for i in range(n_x):
                core_copy(j, i).wait_recv()
            for d in range(1, n_x):
                to = lax.rem(x + d, n_x)
                for g in range(2):
                    x_out[j, d - 1, g] = (
                        part[slot, g, block(to * 2 + core, share), :] + core_in[j, to, g]
                    ).astype(jnp.bfloat16)
                x_copy(j, d).start()
            for g in range(2):
                own[lax.rem(j, LAG + 1), g] = part[slot, g, block(dp, share), :] + core_in[j, x, g]

        @pl.when((k >= 2 * LAG) & (k < steps + 2 * LAG))
        def _():
            j = k - 2 * LAG
            for d in range(1, n_x):
                x_copy(j, d).wait_recv()
            gate, up = own[lax.rem(j, LAG + 1), 0], own[lax.rem(j, LAG + 1), 1]
            for d in range(1, n_x):
                gate += x_in[j, d - 1, 0].astype(jnp.float32)
                up += x_in[j, d - 1, 1].astype(jnp.float32)
            hidden[j, block(dp, share), :] = (gate / (1.0 + jnp.exp(-gate)) * up).astype(jnp.bfloat16)
            for d in range(1, n_x):
                ag_copy(j, d).start()
            sib_copy(j).start()

        @pl.when((k >= 3 * LAG) & (k < steps + 3 * LAG))
        def _():
            j = k - 3 * LAG
            for d in range(1, n_x):
                ag_arrival(j, d).wait_recv()
                fwd_copy(j, d).start()

        @pl.when(k >= 4 * LAG)
        def _():
            j = k - 4 * LAG
            sib_arrival(j).wait_recv()
            for d in range(1, n_x):
                fwd_arrival(j, d).wait_recv()
            h, c = lax.div(j, n), lax.rem(j, n)

            @pl.when(j < n)
            def _():
                down_copy(c).wait()

            product[h] += jnp.dot(hidden[j], down_v[c], preferred_element_type=jnp.float32)
            for h in range(HALVES):
                @pl.when(j == h * n + n - 1)
                def _():
                    send_product(h)

    for h in range(HALVES):
        for d in range(1, n_tp):
            token_copy(h, d).wait_send()

    @pl.loop(0, steps)
    def _(k):
        @pl.when(k + SLOTS >= steps)
        def _():
            for i in range(n_x):
                core_copy(k, i).wait_send()
        for d in range(1, n_x):
            x_copy(k, d).wait_send()
            ag_copy(k, d).wait_send()
            fwd_copy(k, d).wait_send()
        sib_copy(k).wait_send()

    for h in range(HALVES):
        total = product[h, block(rank, slots), :]
        for d in range(1, n_tp):
            z_copy(h, d).wait_recv()
            total += z_in[h, d - 1].astype(jnp.float32)
        out[pl.ds(h * slots, slots), :] = total.astype(jnp.bfloat16)
    for h in range(HALVES):
        for d in range(1, n_tp):
            z_copy(h, d).wait_send()


def solution(mesh):
    n_tp, n_dp = mesh.shape["tp"], mesh.shape["dp"]
    n_x = n_dp // 2

    def on_device(tokens, counts, gate_weight, up_weight, down_weight):
        slots, depth = tokens.shape
        units = gate_weight.shape[1]
        width = chunk_of(units)
        n = units // width
        rows = slots * n_tp // HALVES
        steps = HALVES * n
        share = rows // n_dp
        far = max(n_x - 1, 1)
        dma = pltpu.SemaphoreType.DMA
        mixed = pl.pallas_call(
            functools.partial(kernel, n_tp, n_dp, n, width),
            out_shape=jax.ShapeDtypeStruct((slots, depth), jnp.bfloat16),
            in_specs=[pl.BlockSpec(memory_space=pl.ANY)] * 4,
            out_specs=pl.BlockSpec(memory_space=pltpu.VMEM),
            scratch_shapes=[
                pltpu.VMEM((HALVES, rows, depth), jnp.bfloat16),
                pltpu.VMEM((n, depth, width), jnp.bfloat16),
                pltpu.VMEM((n, depth, width), jnp.bfloat16),
                pltpu.VMEM((n, width, depth), jnp.bfloat16),
                pltpu.VMEM((SLOTS, 2, rows, width), jnp.float32),
                pltpu.VMEM((steps, n_x, 2, share, width), jnp.float32),
                pltpu.VMEM((LAG + 1, 2, share, width), jnp.float32),
                pltpu.VMEM((steps, far, 2, share, width), jnp.bfloat16),
                pltpu.VMEM((steps, far, 2, share, width), jnp.bfloat16),
                pltpu.VMEM((steps, rows, width), jnp.bfloat16),
                pltpu.VMEM((HALVES, rows, depth), jnp.float32),
                pltpu.VMEM((HALVES, n_tp - 1, slots // HALVES, depth), jnp.bfloat16),
                pltpu.VMEM((HALVES, n_tp - 1, slots // HALVES, depth), jnp.bfloat16),
                dma((HALVES,)), dma((HALVES, n_tp - 1)), dma((HALVES, n_tp - 1)),
                dma((n,)), dma((n,)), dma((n,)),
                dma((steps, n_x)), dma((steps, n_x)), dma((steps, far)), dma((steps, far)),
                dma((steps, far)), dma((steps, far)), dma((steps,)), dma((steps,)),
                dma((steps, far)), dma((steps, far)),
                dma((HALVES, n_tp - 1)), dma((HALVES, n_tp - 1)),
            ],
            compiler_params=pltpu.CompilerParams(
                collective_id=0, has_side_effects=True, vmem_limit_bytes=62 * 1024 * 1024
            ),
        )(tokens, gate_weight, up_weight, down_weight)
        live = jnp.arange(slots, dtype=jnp.int32) < counts[0]
        return jnp.where(live[:, None], mixed, jnp.bfloat16(0.0))

    in_specs = (
        P(("groups", "tp"), "dp"),
        P(("groups", "tp")),
        P("dp", "tp"),
        P("dp", "tp"),
        P("tp", "dp"),
    )
    return jax.shard_map(
        on_device, mesh=mesh, in_specs=in_specs, out_specs=P(("groups", "tp"), "dp"), check_vma=False
    )
```

```python
import functools

import jax
import jax.numpy as jnp
from jax import lax
from jax.experimental import pallas as pl
from jax.experimental.pallas import tpu as pltpu
from jax.sharding import PartitionSpec as P

MESH = pl.DeviceIdType.MESH
SLOTS = 4
PAIR, ACT, FORWARD, DOWN = 1, 3, 5, 6
HALVES = 2


def chunk_of(units):
    for width in (768, 512, 384, 256, 128):
        if units % width == 0:
            return width
    return units


def kernel(
    n_tp, n_dp, n, width,
    tokens, gate_w, up_w, down_w, out,
    rows_all, gate_v, up_v, down_v, part, core_in, own, x_out, x_in, hidden, product, z_out, z_in,
    tok_local, tok_s, tok_r, gate_s, up_s, down_s, core_s, core_r, x_s, x_r,
    ag_s, ag_r, sib_s, sib_r, fwd_s, fwd_r, z_s, z_r,
):
    rank = lax.axis_index("tp")
    dp = lax.axis_index("dp")
    n_x = n_dp // 2
    x, core = lax.div(dp, 2), lax.rem(dp, 2)
    sibling = x * 2 + 1 - core
    slots = tokens.shape[0] // HALVES
    share = slots * n_tp // n_dp
    steps = HALVES * n

    def x_peer(d):
        return lax.rem(x + d, n_x) * 2 + core

    def block(index, size):
        return pl.ds(pl.multiple_of(index * size, size), size)

    def weight_copies(k):
        columns = pl.ds(pl.multiple_of(k * width, width), width) if n > 1 else pl.ds(0, width)
        return (
            pltpu.make_async_copy(gate_w.at[:, columns], gate_v.at[k], gate_s.at[k]),
            pltpu.make_async_copy(up_w.at[:, columns], up_v.at[k], up_s.at[k]),
        )

    def down_copy(k):
        rows = pl.ds(pl.multiple_of(k * width, width), width) if n > 1 else pl.ds(0, width)
        return pltpu.make_async_copy(down_w.at[rows, :], down_v.at[k], down_s.at[k])

    def token_move(h, d, source):
        return pltpu.make_async_remote_copy(
            src_ref=tokens.at[pl.ds(h * slots, slots)], dst_ref=rows_all.at[h, block(source, slots)],
            send_sem=tok_s.at[h, d - 1], recv_sem=tok_r.at[h, d - 1],
            device_id={"tp": lax.rem(rank + d, n_tp)}, device_id_type=MESH,
        )

    def token_copy(h, d):
        return token_move(h, d, rank)

    def token_arrival(h, d):
        return token_move(h, d, lax.rem(rank + n_tp - d, n_tp))

    def core_copy(k, i):
        return pltpu.make_async_remote_copy(
            src_ref=part.at[lax.rem(k, SLOTS), :, block(i * 2 + 1 - core, share), :],
            dst_ref=core_in.at[k, i],
            send_sem=core_s.at[k, i], recv_sem=core_r.at[k, i],
            device_id={"dp": sibling}, device_id_type=MESH,
        )

    def x_copy(k, d):
        return pltpu.make_async_remote_copy(
            src_ref=x_out.at[k, d - 1], dst_ref=x_in.at[k, d - 1],
            send_sem=x_s.at[k, d - 1], recv_sem=x_r.at[k, d - 1],
            device_id={"dp": x_peer(d)}, device_id_type=MESH,
        )

    def hidden_copy(k, owner, target, send, recv):
        ref = hidden.at[k, block(owner, share), :]
        return pltpu.make_async_remote_copy(
            src_ref=ref, dst_ref=ref, send_sem=send, recv_sem=recv,
            device_id={"dp": target}, device_id_type=MESH,
        )

    def ag_copy(k, d):
        return hidden_copy(k, dp, x_peer(d), ag_s.at[k, d - 1], ag_r.at[k, d - 1])

    def ag_arrival(k, d):
        return hidden_copy(k, x_peer(n_x - d), x_peer(d), ag_s.at[k, d - 1], ag_r.at[k, d - 1])

    def sib_copy(k):
        return hidden_copy(k, dp, sibling, sib_s.at[k], sib_r.at[k])

    def sib_arrival(k):
        return hidden_copy(k, sibling, sibling, sib_s.at[k], sib_r.at[k])

    def fwd_copy(k, d):
        return hidden_copy(k, x_peer(n_x - d), sibling, fwd_s.at[k, d - 1], fwd_r.at[k, d - 1])

    def fwd_arrival(k, d):
        owner = lax.rem(x + n_x - d, n_x) * 2 + 1 - core
        return hidden_copy(k, owner, sibling, fwd_s.at[k, d - 1], fwd_r.at[k, d - 1])

    def z_copy(h, d):
        return pltpu.make_async_remote_copy(
            src_ref=z_out.at[h, d - 1], dst_ref=z_in.at[h, d - 1],
            send_sem=z_s.at[h, d - 1], recv_sem=z_r.at[h, d - 1],
            device_id={"tp": lax.rem(rank + d, n_tp)}, device_id_type=MESH,
        )

    def send_product(h):
        for d in range(1, n_tp):
            z_out[h, d - 1] = product[h, block(lax.rem(rank + d, n_tp), slots), :].astype(jnp.bfloat16)
            z_copy(h, d).start()

    own_rows = [
        pltpu.make_async_copy(
            tokens.at[pl.ds(h * slots, slots)], rows_all.at[h, block(rank, slots)], tok_local.at[h]
        )
        for h in range(HALVES)
    ]
    for copy in own_rows:
        copy.start()

    barrier = pltpu.get_barrier_semaphore()
    for d in range(1, n_tp):
        pl.semaphore_signal(barrier, inc=1, device_id={"tp": lax.rem(rank + d, n_tp)}, device_id_type=MESH)
    for d in range(1, n_x):
        pl.semaphore_signal(barrier, inc=1, device_id={"dp": x_peer(d)}, device_id_type=MESH)
    pl.semaphore_signal(barrier, inc=1, device_id={"dp": sibling}, device_id_type=MESH)

    @pl.loop(0, n)
    def _(k):
        for copy in weight_copies(k):
            copy.start()

    pl.semaphore_wait(barrier, n_tp - 1 + n_x)
    for d in range(1, n_tp):
        token_copy(0, d).start()

    @pl.loop(0, n)
    def _(k):
        down_copy(k).start()

    product[...] = jnp.zeros_like(product)
    for copy in own_rows:
        copy.wait()
    for d in range(1, n_tp):
        token_arrival(0, d).wait_recv()
    for h in range(1, HALVES):
        for d in range(1, n_tp):
            token_copy(h, d).start()

    @pl.loop(0, steps + DOWN)
    def _(k):
        @pl.when(k < steps)
        def _():
            @pl.when(k >= SLOTS)
            def _():
                for i in range(n_x):
                    core_copy(k - SLOTS, i).wait_send()

            for h in range(1, HALVES):
                @pl.when(k == h * n)
                def _():
                    for d in range(1, n_tp):
                        token_arrival(h, d).wait_recv()

            slot, h, c = lax.rem(k, SLOTS), lax.div(k, n), lax.rem(k, n)

            @pl.when(k < n)
            def _():
                for copy in weight_copies(c):
                    copy.wait()

            part[slot, 0] = jnp.dot(rows_all[h], gate_v[c], preferred_element_type=jnp.float32)
            part[slot, 1] = jnp.dot(rows_all[h], up_v[c], preferred_element_type=jnp.float32)
            for i in range(n_x):
                core_copy(k, i).start()

        @pl.when((k >= PAIR) & (k < steps + PAIR))
        def _():
            j = k - PAIR
            slot = lax.rem(j, SLOTS)
            for i in range(n_x):
                core_copy(j, i).wait_recv()
            for d in range(1, n_x):
                to = lax.rem(x + d, n_x)
                for g in range(2):
                    x_out[j, d - 1, g] = (
                        part[slot, g, block(to * 2 + core, share), :] + core_in[j, to, g]
                    ).astype(jnp.bfloat16)
                x_copy(j, d).start()
            for g in range(2):
                own[lax.rem(j, ACT - PAIR + 1), g] = part[slot, g, block(dp, share), :] + core_in[j, x, g]

        @pl.when((k >= ACT) & (k < steps + ACT))
        def _():
            j = k - ACT
            for d in range(1, n_x):
                x_copy(j, d).wait_recv()
            gate, up = own[lax.rem(j, ACT - PAIR + 1), 0], own[lax.rem(j, ACT - PAIR + 1), 1]
            for d in range(1, n_x):
                gate += x_in[j, d - 1, 0].astype(jnp.float32)
                up += x_in[j, d - 1, 1].astype(jnp.float32)
            hidden[j, block(dp, share), :] = (gate / (1.0 + jnp.exp(-gate)) * up).astype(jnp.bfloat16)
            for d in range(1, n_x):
                ag_copy(j, d).start()
            sib_copy(j).start()

        @pl.when((k >= FORWARD) & (k < steps + FORWARD))
        def _():
            j = k - FORWARD
            for d in range(1, n_x):
                ag_arrival(j, d).wait_recv()
                fwd_copy(j, d).start()

        @pl.when(k >= DOWN)
        def _():
            j = k - DOWN
            sib_arrival(j).wait_recv()
            for d in range(1, n_x):
                fwd_arrival(j, d).wait_recv()
            h, c = lax.div(j, n), lax.rem(j, n)

            @pl.when(j < n)
            def _():
                down_copy(c).wait()

            product[h] += jnp.dot(hidden[j], down_v[c], preferred_element_type=jnp.float32)
            for h in range(HALVES):
                @pl.when(j == h * n + n - 1)
                def _():
                    send_product(h)

    for h in range(HALVES):
        for d in range(1, n_tp):
            token_copy(h, d).wait_send()

    @pl.loop(0, steps)
    def _(k):
        @pl.when(k + SLOTS >= steps)
        def _():
            for i in range(n_x):
                core_copy(k, i).wait_send()
        for d in range(1, n_x):
            x_copy(k, d).wait_send()
            ag_copy(k, d).wait_send()
            fwd_copy(k, d).wait_send()
        sib_copy(k).wait_send()

    for h in range(HALVES):
        total = product[h, block(rank, slots), :]
        for d in range(1, n_tp):
            z_copy(h, d).wait_recv()
            total += z_in[h, d - 1].astype(jnp.float32)
        out[pl.ds(h * slots, slots), :] = total.astype(jnp.bfloat16)
    for h in range(HALVES):
        for d in range(1, n_tp):
            z_copy(h, d).wait_send()


def solution(mesh):
    n_tp, n_dp = mesh.shape["tp"], mesh.shape["dp"]
    n_x = n_dp // 2

    def on_device(tokens, counts, gate_weight, up_weight, down_weight):
        slots, depth = tokens.shape
        units = gate_weight.shape[1]
        width = chunk_of(units)
        n = units // width
        rows = slots * n_tp // HALVES
        steps = HALVES * n
        share = rows // n_dp
        far = max(n_x - 1, 1)
        dma = pltpu.SemaphoreType.DMA
        mixed = pl.pallas_call(
            functools.partial(kernel, n_tp, n_dp, n, width),
            out_shape=jax.ShapeDtypeStruct((slots, depth), jnp.bfloat16),
            in_specs=[pl.BlockSpec(memory_space=pl.ANY)] * 4,
            out_specs=pl.BlockSpec(memory_space=pltpu.VMEM),
            scratch_shapes=[
                pltpu.VMEM((HALVES, rows, depth), jnp.bfloat16),
                pltpu.VMEM((n, depth, width), jnp.bfloat16),
                pltpu.VMEM((n, depth, width), jnp.bfloat16),
                pltpu.VMEM((n, width, depth), jnp.bfloat16),
                pltpu.VMEM((SLOTS, 2, rows, width), jnp.float32),
                pltpu.VMEM((steps, n_x, 2, share, width), jnp.float32),
                pltpu.VMEM((ACT - PAIR + 1, 2, share, width), jnp.float32),
                pltpu.VMEM((steps, far, 2, share, width), jnp.bfloat16),
                pltpu.VMEM((steps, far, 2, share, width), jnp.bfloat16),
                pltpu.VMEM((steps, rows, width), jnp.bfloat16),
                pltpu.VMEM((HALVES, rows, depth), jnp.float32),
                pltpu.VMEM((HALVES, n_tp - 1, slots // HALVES, depth), jnp.bfloat16),
                pltpu.VMEM((HALVES, n_tp - 1, slots // HALVES, depth), jnp.bfloat16),
                dma((HALVES,)), dma((HALVES, n_tp - 1)), dma((HALVES, n_tp - 1)),
                dma((n,)), dma((n,)), dma((n,)),
                dma((steps, n_x)), dma((steps, n_x)), dma((steps, far)), dma((steps, far)),
                dma((steps, far)), dma((steps, far)), dma((steps,)), dma((steps,)),
                dma((steps, far)), dma((steps, far)),
                dma((HALVES, n_tp - 1)), dma((HALVES, n_tp - 1)),
            ],
            compiler_params=pltpu.CompilerParams(
                collective_id=0, has_side_effects=True, vmem_limit_bytes=62 * 1024 * 1024
            ),
        )(tokens, gate_weight, up_weight, down_weight)
        live = jnp.arange(slots, dtype=jnp.int32) < counts[0]
        return jnp.where(live[:, None], mixed, jnp.bfloat16(0.0))

    in_specs = (
        P(("groups", "tp"), "dp"),
        P(("groups", "tp")),
        P("dp", "tp"),
        P("dp", "tp"),
        P("tp", "dp"),
    )
    return jax.shard_map(
        on_device, mesh=mesh, in_specs=in_specs, out_specs=P(("groups", "tp"), "dp"), check_vma=False
    )
```
